128 devices in a mesh: pool: 4 (over x), ep: 32 (over y, z, core).
Axes of the slice: x: 4, y: 4, z: 4, core: 2. Of those that a mesh axis runs over, the one named last changes fastest.
Arguments:
- tokens: bfloat16 [16384, 4096], P(('pool', 'ep')), may hold values from -6 to 6
- modality: int32 [16384], P(('pool', 'ep')), may hold values from 0 to 1, as said below
- chosen: int32 [32, 512], replicated, may hold values from 0 to 16383, as said below
- gates: float32 [32, 512], P('ep'), may hold values from 0.1 to 1
- w_gate: bfloat16 [32, 4096, 1024], P('ep', None, 'pool'), may hold values from -0.09375 to 0.09375
- w_up: bfloat16 [32, 4096, 1024], P('ep', None, 'pool'), may hold values from -0.09375 to 0.09375
- w_down: bfloat16 [32, 1024, 4096], P('ep', 'pool'), may hold values from -0.1875 to 0.1875
- cotangent: bfloat16 [16384, 4096], P(('pool', 'ep')), may hold values from -6 to 6
Outputs:
- mixed: bfloat16 [16384, 4096], P(('pool', 'ep'))
- token_grad: bfloat16 [16384, 4096], P(('pool', 'ep'))
- gate_grad: float32 [32, 512], P('ep')
- w_gate_grad: float32 [32, 4096, 1024], P('ep', None, 'pool')
- w_up_grad: float32 [32, 4096, 1024], P('ep', None, 'pool')
- w_down_grad: float32 [32, 1024, 4096], P('ep', 'pool')
The draws below stay inside these ranges and needn't reach their ends.
Inputs may be any that keep to these rules, and one draw needn't show every extreme that they name: Every device's 128 tokens (device i holding tokens i * 128 to (i + 1) * 128 - 1) hold at least 8 tokens of each modality. `chosen`: row e lists 512 different tokens in increasing order; at most 8 of a row fall among one device's 128 tokens, and for every row exactly 8 do in some device.
All inputs are finite; a program needn't handle non-finite values.
Results may differ from the reference program's by a relative error of at most 0.0095.
Values may be sent and summed in bfloat16 or wider, within the bound.
No kernel may reach another device: no remote copies, remote signals or barrier semaphores. Data moves between devices by JAX's collectives and lax.ppermute only.
A program may use at most 128 MiB of HBM per device.

```python
import math
import jax
import jax.numpy as jnp
from jax import lax

D = 4096
FF = 1024
TOK_DEV = 128
EXPERTS = 32
TEXT_EXP = 24
CAP = 512
SLOT = 8
TOKENS = 16384
N_POOL = 4
N_EP = 32


def shared_layout(key):
    device_count = N_POOL * N_EP
    keys = jax.random.split(key, 6)
    level = jax.random.randint(keys[0], (device_count, 1), 1, 8)
    coins = jax.random.randint(keys[1], (device_count, TOK_DEV), 0, 8)
    image = coins < level
    places = jax.vmap(lambda one: jax.random.permutation(one, TOK_DEV))(jax.random.split(keys[2], device_count))
    image = jnp.where(places < SLOT, True, jnp.where(places < 2 * SLOT, False, image))
    modality = image.astype(jnp.int32).reshape(TOKENS)
    scores = jax.vmap(lambda one: jax.random.permutation(one, TOKENS))(jax.random.split(keys[3], EXPERTS)).astype(jnp.int32)
    expert_kind = (jnp.arange(EXPERTS) >= TEXT_EXP).astype(jnp.int32)
    fits = modality[None, :] == expert_kind[:, None]
    stray = jax.random.randint(keys[5], (EXPERTS, TOKENS), 0, 8) == 0
    allowed = fits | stray
    masked = jnp.where(allowed, scores, -1).reshape(EXPERTS, device_count, TOK_DEV)
    order = jnp.argsort(-masked, axis=2, stable=True)
    ranks = jnp.argsort(order, axis=2, stable=True)
    eligible = allowed.reshape(EXPERTS, device_count, TOK_DEV) & (ranks < SLOT)
    favored = jax.random.randint(keys[4], (EXPERTS,), 0, device_count)
    boost = (jnp.arange(device_count)[None, :] == favored[:, None]).astype(jnp.int32)[:, :, None] * TOKENS
    final = jnp.where(eligible, masked + boost, -1).reshape(EXPERTS, TOKENS)
    _, picked = lax.top_k(final, CAP)
    chosen = jnp.sort(picked.astype(jnp.int32), axis=1)
    return (modality, chosen)


def draw_modality(key, part):
    modality, chosen = shared_layout(key)
    return modality


def draw_chosen(key, part):
    modality, chosen = shared_layout(key)
    return chosen


def level_of(stream_key, dims, pieces, least, largest):
    def one(position, shards_of):
        heights = jax.random.uniform(jax.random.fold_in(jax.random.fold_in(stream_key, 6), position), (shards_of,), jnp.float32, least / len(pieces), largest / len(pieces))
        return jnp.repeat(jnp.exp(heights), dims[position] // shards_of).reshape((-1,) + (1,) * (len(dims) - position - 1))

    gain = one(*pieces[0])
    for cut in pieces[1:]:
        gain = gain * one(*cut)
    return gain


def centred(key, extent, deviation, most, shards=(), dtype=jnp.bfloat16):
    gain = level_of(key, extent, shards, -0.22, 0.18) if shards else 1.0
    array = jax.random.normal(key, extent, jnp.float32) * deviation * gain
    return jnp.minimum(jnp.maximum(array, -most), most).astype(dtype)


def setup_inputs(seed: int = 0) -> dict:
    seeds = jax.random.split(jax.random.key(seed), 9)
    return {
        "tokens": centred(seeds[0], (TOKENS, D), 1.0, 6.0, ((0, 128),)),
        "modality": draw_modality(jax.random.fold_in(seeds[8], 71), 0),
        "chosen": draw_chosen(jax.random.fold_in(seeds[8], 71), 0),
        "gates": jnp.clip(jnp.exp(math.log(1.0) - 2.3025851 * jax.random.uniform(seeds[3], (EXPERTS, CAP), jnp.float32) ** level_of(seeds[3], (EXPERTS, CAP), ((0, 32),), -0.2, 0.2)), 0.1, 1.0),
        "w_gate": centred(seeds[4], (EXPERTS, D, FF), D ** -0.5, 0.09375, ((0, 32), (2, 4))),
        "w_up": centred(seeds[5], (EXPERTS, D, FF), D ** -0.5, 0.09375, ((0, 32), (2, 4))),
        "w_down": centred(seeds[6], (EXPERTS, FF, D), FF ** -0.5, 0.1875, ((0, 32), (1, 4))),
        "cotangent": centred(seeds[7], (TOKENS, D), 1.0, 6.0, ((0, 128),)),
    }


def reference(tokens, modality, chosen, gates, w_gate, w_up, w_down, cotangent):
    expert_total = chosen.shape[0]
    hidden_total = w_gate.shape[2]
    share = hidden_total // N_POOL
    kinds = (jnp.arange(expert_total) >= TEXT_EXP).astype(jnp.int32)

    def per_expert(carry, inputs):
        acc_out, acc_in = carry
        row_ids, gate_row, kind, wg, wu, wd = inputs
        match = (modality[row_ids] == kind).astype(jnp.float32)
        weight = gate_row * match
        inputs_e = tokens[row_ids]
        grads_e = cotangent[row_ids]
        gate_pre = jnp.dot(inputs_e, wg, preferred_element_type=jnp.float32)
        up_pre = jnp.dot(inputs_e, wu, preferred_element_type=jnp.float32)
        sig = jax.nn.sigmoid(gate_pre)
        act = gate_pre * sig
        hidden = (act * up_pre).astype(jnp.bfloat16)
        out_grad = (weight[:, None] * grads_e.astype(jnp.float32)).astype(jnp.bfloat16)
        wd_grad = jnp.dot(hidden.T, out_grad, preferred_element_type=jnp.float32)
        hidden_grad = jnp.dot(out_grad, wd.T, preferred_element_type=jnp.float32)
        gate_back = (hidden_grad * up_pre * (sig * (1.0 + gate_pre * (1.0 - sig)))).astype(jnp.bfloat16)
        up_back = (hidden_grad * act).astype(jnp.bfloat16)
        wg_grad = jnp.dot(inputs_e.T, gate_back, preferred_element_type=jnp.float32)
        wu_grad = jnp.dot(inputs_e.T, up_back, preferred_element_type=jnp.float32)
        gate_sum = jnp.zeros(row_ids.shape, jnp.float32)
        for index in range(N_POOL):
            lower = index * share
            upper = lower + share
            part = jnp.dot(hidden[:, lower:upper], wd[lower:upper], preferred_element_type=jnp.float32)
            share_out = lax.optimization_barrier((weight[:, None] * part).astype(jnp.bfloat16))
            acc_out = acc_out.at[row_ids].add(share_out.astype(jnp.float32))
            gate_sum = gate_sum + jnp.sum(grads_e.astype(jnp.float32) * part, axis=1)
            share_in = jnp.dot(gate_back[:, lower:upper], wg[:, lower:upper].T, preferred_element_type=jnp.float32)
            share_in = share_in + jnp.dot(up_back[:, lower:upper], wu[:, lower:upper].T, preferred_element_type=jnp.float32)
            share_in = lax.optimization_barrier(share_in.astype(jnp.bfloat16))
            acc_in = acc_in.at[row_ids].add(share_in.astype(jnp.float32))
        return (acc_out, acc_in), (gate_sum * match, wg_grad, wu_grad, wd_grad)

    start = jnp.zeros(tokens.shape, jnp.float32)
    (acc_out, acc_in), (gate_grad, wg_all, wu_all, wd_all) = lax.scan(
        per_expert, (start, start), (chosen, gates, kinds, w_gate, w_up, w_down))
    return (acc_out.astype(jnp.bfloat16), acc_in.astype(jnp.bfloat16), gate_grad, wg_all, wu_all, wd_all)
```

```python
import jax
import jax.numpy as jnp
from jax import lax
from jax.sharding import PartitionSpec as P

BF16 = jnp.bfloat16
F32 = jnp.float32
BOTH = ("pool", "ep")


def dot(a, b, dims, out=F32):
    return lax.dot_general(a, b, ((dims[0], dims[1]), ((), ())), preferred_element_type=out)


def shift(value, step):
    size = lax.axis_size("pool")
    return lax.ppermute(value, "pool", [(i, (i + step) % size) for i in range(size)])


def gather_ring(block):
    rows, cols = block.shape
    half = rows // 2
    me = lax.axis_index("pool")
    size = lax.axis_size("pool")
    left = shift(block, 1)
    right = shift(block, -1)
    far_top = shift(left[:half], 1)
    far_low = shift(right[half:], -1)
    whole = jnp.zeros((rows, size * cols), block.dtype)
    far = jnp.concatenate([far_top, far_low], axis=0)
    for step, piece in ((0, block), (-1, left), (1, right), (2, far)):
        whole = lax.dynamic_update_slice(whole, piece, (0, (me + step) % size * cols))
    return whole


def scatter_ring(whole):
    rows, width = whole.shape
    size = lax.axis_size("pool")
    cols = width // size
    half = rows // 2
    me = lax.axis_index("pool")

    def block(step):
        return lax.dynamic_slice(whole, (0, (me + step) % size * cols), (rows, cols))

    def add(a, b):
        return (a.astype(F32) + b.astype(F32)).astype(BF16)

    far = block(2)
    from_left = shift(far[:half], 1)
    from_right = shift(far[half:], -1)
    ahead, behind = block(1), block(-1)
    from_left = shift(jnp.concatenate([add(ahead[:half], from_left), ahead[half:]], axis=0), 1)
    from_right = shift(jnp.concatenate([behind[:half], add(behind[half:], from_right)], axis=0), -1)
    return (block(0).astype(F32) + from_left.astype(F32) + from_right.astype(F32)).astype(BF16)


def exchange(blocks):
    return lax.all_to_all(blocks, BOTH, split_axis=0, concat_axis=0, tiled=True)


def body(tokens, modality, chosen, gates, w_gate, w_up, w_down, cotangent):
    tok_rows, width = tokens.shape
    pool_size = lax.axis_size("pool")
    ep_size = lax.axis_size("ep")
    devices = pool_size * ep_size
    slots = 2 * tok_rows // ep_size
    capacity = chosen.shape[1]
    text_count = 3 * ep_size // 4
    cols = width // pool_size
    expert = lax.axis_index("ep")
    source = lax.axis_index("pool") * ep_size + expert

    local = chosen - source * tok_rows
    below = jnp.sum((local < 0).astype(jnp.int32), axis=1, keepdims=True)
    inside = (local >= 0) & (local < tok_rows)
    place = jnp.where(inside, jnp.arange(capacity, dtype=jnp.int32)[None, :] - below, -1)
    at_slot = place[:, None, :] == jnp.arange(slots, dtype=jnp.int32)[None, :, None]
    token_at = jnp.sum(jnp.where(at_slot, local[:, None, :] + 1, 0), axis=2) - 1
    token_at = token_at.reshape(ep_size * slots, 1)
    kind = (jnp.arange(ep_size * slots, dtype=jnp.int32) >= text_count * slots).astype(jnp.int32)
    pick = (token_at == jnp.arange(tok_rows, dtype=jnp.int32)[None, :]) & (
        kind[:, None] == modality[None, :]
    )
    pick = pick.astype(BF16)

    picks = lax.dynamic_slice_in_dim(chosen, expert, 1, 0)[0]
    holder = picks // tok_rows
    order = jnp.arange(capacity, dtype=jnp.int32)
    same = (holder[:, None] == holder[None, :]) & (order[None, :] < order[:, None])
    flat = holder * slots + jnp.sum(same.astype(jnp.int32), axis=1)
    place_in = (flat[:, None] == jnp.arange(devices * slots, dtype=jnp.int32)[None, :]).astype(BF16)

    def fetch(rows):
        parts = [
            dot(pick, rows[:, q * cols : (q + 1) * cols], ((1,), (0,)), BF16)
            for q in range(pool_size)
        ]
        got = exchange(jnp.stack(parts).reshape(devices, slots, cols))
        return dot(place_in, got.reshape(devices * slots, cols), ((1,), (0,)), BF16)

    def deliver(block):
        buffer = dot(place_in, block, ((0,), (0,)), BF16)
        got = exchange(buffer.reshape(devices, slots, cols)).reshape(pool_size, -1, cols)
        return jnp.concatenate(
            [dot(pick, got[q], ((0,), (0,)), BF16) for q in range(pool_size)], axis=1
        )

    wg, wu, wd = w_gate[0], w_up[0], w_down[0]
    weight = gates[0][:, None]
    inputs = gather_ring(fetch(tokens))
    grads = gather_ring(fetch(cotangent))

    gate_pre = dot(inputs, wg, ((1,), (0,)))
    up_pre = dot(inputs, wu, ((1,), (0,)))
    sig = jax.nn.sigmoid(gate_pre)
    act = gate_pre * sig
    hidden = (act * up_pre).astype(BF16)
    share_out = (weight * dot(hidden, wd, ((1,), (0,)))).astype(BF16)
    mixed = deliver(scatter_ring(share_out))

    back = dot(grads, wd, ((1,), (1,)))
    gate_grad = lax.psum(jnp.sum(back * hidden.astype(F32), axis=1), "pool")[None, :]
    hidden_grad = weight * back
    gate_back = (hidden_grad * up_pre * (sig * (1.0 + gate_pre * (1.0 - sig)))).astype(BF16)
    up_back = (hidden_grad * act).astype(BF16)
    share_in = dot(gate_back, wg, ((1,), (1,))) + dot(up_back, wu, ((1,), (1,)))
    token_grad = deliver(scatter_ring(share_in.astype(BF16)))

    scaled = (weight * hidden.astype(F32)).astype(BF16)
    wd_grad = dot(scaled, grads, ((0,), (0,)))
    wg_grad = dot(inputs, gate_back, ((0,), (0,)))
    wu_grad = dot(inputs, up_back, ((0,), (0,)))
    return (mixed, token_grad, gate_grad, wg_grad[None], wu_grad[None], wd_grad[None])


def solution(mesh):
    return jax.shard_map(
        body,
        mesh=mesh,
        in_specs=(
            P(BOTH, None),
            P(BOTH),
            P(),
            P("ep", None),
            P("ep", None, "pool"),
            P("ep", None, "pool"),
            P("ep", "pool", None),
            P(BOTH, None),
        ),
        out_specs=(
            P(BOTH, None),
            P(BOTH, None),
            P("ep", None),
            P("ep", None, "pool"),
            P("ep", None, "pool"),
            P("ep", "pool", None),
        ),
        check_vma=False,
    )
```

```python
import jax
import jax.numpy as jnp
from jax import lax
from jax.experimental import pallas as pl
from jax.experimental.pallas import tpu as pltpu
from jax.sharding import PartitionSpec as P

BF16 = jnp.bfloat16
F32 = jnp.float32
BOTH = ("pool", "ep")
ROW_COL = ((1,), (0,))
COL_COL = ((1,), (1,))
ROW_ROW = ((0,), (0,))


def dot(a, b, dims, out=F32):
    return lax.dot_general(a, b, (dims, ((), ())), preferred_element_type=out)


def add(*terms):
    total = terms[0].astype(F32)
    for term in terms[1:]:
        total = total + term.astype(F32)
    return total


def shift(value, step):
    size = lax.axis_size("pool")
    return lax.ppermute(value, "pool", [(i, (i + step) % size) for i in range(size)])


def after(value, *earlier):
    return lax.optimization_barrier((value, *earlier))[0]


def swap(get):
    behind = shift(get(-1), -1)
    before = shift(get(1), 1)
    far = shift(get(2), 2)
    return [get(0), behind, far, before]


def spread(block):
    return swap(lambda d: block)


def ring_gather(block):
    half = block.shape[0] // 2
    top, low = block[:half], block[half:]
    before_top, behind_low = shift(top, 1), shift(low, -1)
    before_low, behind_top = shift(low, 1), shift(top, -1)
    far_top, far_low = shift(before_top, 1), shift(behind_low, -1)
    pairs = ((behind_top, behind_low), (far_top, far_low), (before_top, before_low))
    return [block, *(jnp.concatenate(pair, axis=0) for pair in pairs)]


def ring_sum(get):
    far, ahead, back = get(2), get(1), get(-1)
    half = far.shape[0] // 2
    first_up = jnp.concatenate([far[:half], ahead[half:]], axis=0).astype(BF16)
    first_down = jnp.concatenate([back[:half], far[half:]], axis=0).astype(BF16)
    up = shift(first_up, 1)
    down = shift(first_down, -1)
    second_up = add(ahead[:half], up[:half]).astype(BF16)
    second_down = add(back[half:], down[half:]).astype(BF16)
    up_top = shift(second_up, 1)
    down_low = shift(second_down, -1)
    total = add(
        get(0),
        jnp.concatenate([up_top, up[half:]], axis=0),
        jnp.concatenate([down[:half], down_low], axis=0),
    )
    return total, (second_up, second_down)


def thirds(value):
    high = lax.optimization_barrier(value.astype(BF16))
    rest = value - high.astype(F32)
    middle = lax.optimization_barrier(rest.astype(BF16))
    return high, middle, (rest - middle.astype(F32)).astype(BF16)


def masked_send(pick, parts, text_rows):
    total, held = pick.shape
    rows = held // len(parts)
    cols = parts[0].shape[1]
    tile = total // 4

    def kernel(pick_ref, *refs):
        part_refs, out_ref, values, kinds = refs[: len(parts)], refs[-3], refs[-2], refs[-1]
        step = pl.program_id(0)

        @pl.when(step == 0)
        def _():
            for d, ref in enumerate(part_refs):
                values[d * rows : (d + 1) * rows, :] = ref[:rows, :]
                kinds[:, d * rows : (d + 1) * rows] = ref[rows:, :rows]

        kind = kinds[:1, :].astype(F32)
        row = step * tile + lax.broadcasted_iota(jnp.int32, (tile, 1), 0)
        keep = jnp.where(row < text_rows, 1.0 - kind, kind)
        chosen = (pick_ref[...].astype(F32) * keep).astype(BF16)
        out_ref[...] = dot(chosen, values[...], ROW_COL).astype(BF16)

    return pl.pallas_call(
        kernel,
        grid=(4,),
        out_shape=jax.ShapeDtypeStruct((total, cols), BF16),
        in_specs=[pl.BlockSpec((tile, held), lambda i: (i, 0))]
        + [pl.BlockSpec(part.shape, lambda i: (0, 0)) for part in parts],
        out_specs=pl.BlockSpec((tile, cols), lambda i: (i, 0)),
        scratch_shapes=[pltpu.VMEM((held, cols), BF16), pltpu.VMEM((16, held), BF16)],
        cost_estimate=pl.CostEstimate(
            flops=2 * total * held * cols, bytes_accessed=2 * (total * cols * 2 + total * held), transcendentals=0
        ),
        compiler_params=pltpu.CompilerParams(vmem_limit_bytes=24 * 1024 * 1024),
    )(pick, *parts)


def assemble(parts, members, dtype):
    rows, cols = parts[0].shape

    def kernel(members_ref, *refs):
        for d, ref in enumerate(refs[:-1]):

            @pl.when(pl.program_id(0) == d)
            def _(ref=ref):
                refs[-1][...] = ref[...].astype(dtype)

    return pl.pallas_call(
        kernel,
        grid_spec=pltpu.PrefetchScalarGridSpec(
            num_scalar_prefetch=1,
            grid=(len(parts),),
            in_specs=[pl.BlockSpec((rows, cols), lambda d, m: (0, 0)) for _ in parts],
            out_specs=pl.BlockSpec((rows, cols), lambda d, m: (0, m[d])),
        ),
        out_shape=jax.ShapeDtypeStruct((rows, len(parts) * cols), dtype),
        cost_estimate=pl.CostEstimate(
            flops=0, bytes_accessed=len(parts) * rows * cols * (2 + jnp.dtype(dtype).itemsize), transcendentals=0
        ),
        compiler_params=pltpu.CompilerParams(vmem_limit_bytes=24 * 1024 * 1024),
    )(members, *parts)


def weight_grads(inputs, members, gate_back, up_back):
    count, cols = inputs[0].shape
    share = gate_back.shape[1]

    def kernel(members_ref, *refs):
        blocks, (gate_ref, up_ref, gate_out, up_out) = refs[:-4], refs[-4:]
        for d, ref in enumerate(blocks):

            @pl.when(pl.program_id(0) == d)
            def _(ref=ref):
                gate_out[...] = dot(ref[...], gate_ref[...], ROW_ROW)
                up_out[...] = dot(ref[...], up_ref[...], ROW_ROW)

    whole = jax.ShapeDtypeStruct((len(inputs) * cols, share), F32)
    return pl.pallas_call(
        kernel,
        grid_spec=pltpu.PrefetchScalarGridSpec(
            num_scalar_prefetch=1,
            grid=(len(inputs),),
            in_specs=[pl.BlockSpec((count, cols), lambda d, m: (0, 0)) for _ in inputs]
            + [pl.BlockSpec((count, share), lambda d, m: (0, 0))] * 2,
            out_specs=[pl.BlockSpec((cols, share), lambda d, m: (m[d], 0))] * 2,
        ),
        out_shape=[whole, whole],
        cost_estimate=pl.CostEstimate(
            flops=4 * count * cols * share * len(inputs),
            bytes_accessed=len(inputs) * (count * cols * 2 + cols * share * 8),
            transcendentals=0,
        ),
        compiler_params=pltpu.CompilerParams(vmem_limit_bytes=32 * 1024 * 1024),
    )(members, *inputs, gate_back, up_back)


def body(tokens, modality, chosen, gates, w_gate, w_up, w_down, cotangent):
    tok_rows, width = tokens.shape
    size = lax.axis_size("pool")
    ep_size = lax.axis_size("ep")
    slots = 2 * tok_rows // ep_size
    capacity = chosen.shape[1]
    text_count = 3 * ep_size // 4
    cols = width // size
    share = w_gate.shape[2]
    me = lax.axis_index("pool")
    mine = lax.axis_index("ep")
    members = [(me + d) % size for d in range(size)]
    pool_order = jnp.stack(members).astype(jnp.int32)

    def columns(array):
        return lambda d: lax.dynamic_slice(
            array, (0, members[d % size] * cols), (array.shape[0], cols)
        )

    def rows(array, count):
        return lambda d: lax.dynamic_slice(
            array, (members[d % size] * count, 0), (count, array.shape[1])
        )

    extra = jnp.broadcast_to(jnp.pad(modality, (0, cols - tok_rows)).astype(BF16), (16, cols))
    token_parts = swap(lambda d: jnp.concatenate([columns(tokens)(d), extra], axis=0))
    grad_parts = swap(columns(cotangent))
    down_parts = swap(columns(after(w_down[0], *grad_parts[1:])))
    down = jnp.concatenate(down_parts, axis=0)

    token_at = []
    for d in range(size):
        first = (members[d] * ep_size + mine) * tok_rows
        local = chosen - first
        below = jnp.sum((local < 0).astype(jnp.int32), axis=1, keepdims=True)
        inside = (local >= 0) & (local < tok_rows)
        place = jnp.where(inside, jnp.arange(capacity, dtype=jnp.int32)[None, :] - below, -1)
        at_slot = place[:, None, :] == jnp.arange(slots, dtype=jnp.int32)[None, :, None]
        held = jnp.sum(jnp.where(at_slot, local[:, None, :] + 1, 0), axis=2) - 1
        token_at.append(jnp.where(held < 0, -1, held + d * tok_rows))
    token_at = jnp.stack(token_at, axis=1).reshape(ep_size * size * slots, 1)
    token_ids = jnp.arange(size * tok_rows, dtype=jnp.int32)
    pick = (token_at == token_ids[None, :]).astype(BF16)
    pick_back = (token_at.reshape(1, -1) == token_ids[:, None]).astype(BF16)
    pick, pick_back = lax.optimization_barrier((pick, pick_back))

    picks = lax.dynamic_slice_in_dim(chosen, mine, 1, 0)[0]
    holder = picks // tok_rows
    order = jnp.arange(capacity, dtype=jnp.int32)
    same = (holder[:, None] == holder[None, :]) & (order[None, :] < order[:, None])
    rank = jnp.sum(same.astype(jnp.int32), axis=1)
    pool_of, ep_of = holder // ep_size, holder % ep_size
    flat = (ep_of * size + (pool_of - me) % size) * slots + rank
    slot_total = ep_size * size * slots
    slot_ids = jnp.arange(slot_total, dtype=jnp.int32)
    place_in = (flat[:, None] == slot_ids[None, :]).astype(BF16)
    place_out = (flat[None, :] == slot_ids[:, None]).astype(BF16)
    place_in, place_out = lax.optimization_barrier((place_in, place_out))

    def exchange(values):
        blocks = values.reshape(ep_size, size * slots, cols)
        blocks = lax.all_to_all(blocks, "ep", split_axis=0, concat_axis=0, tiled=True)
        return blocks.reshape(slot_total, cols)

    def fetch(sent):
        return dot(place_in, exchange(sent), ROW_COL, BF16)

    def carry(block):
        return exchange(dot(place_out, block, ROW_COL, BF16))

    def collect(got):
        summed = dot(pick_back, got, ROW_COL, BF16)
        return swap(lambda d: summed[d % size * tok_rows : (d % size + 1) * tok_rows])

    wg, wu = w_gate[0], w_up[0]
    weight = gates[0][:, None]
    sent = masked_send(pick, token_parts, text_count * size * slots)
    block = fetch(after(sent, grad_parts[1], grad_parts[3]))
    block = after(block, *down_parts)
    inputs = ring_gather(block)
    sent = dot(pick, jnp.concatenate(grad_parts, axis=0), ROW_COL, BF16)
    grads = fetch(after(sent, block))

    gate_pre = sum(dot(inputs[d], rows(wg, cols)(d), ROW_COL) for d in (0, 1, 3, 2))
    up_pre = sum(dot(inputs[d], rows(wu, cols)(d), ROW_COL) for d in (0, 1, 3, 2))
    sig = jax.nn.sigmoid(gate_pre)
    act = gate_pre * sig
    hidden = (act * up_pre).astype(BF16)

    back_own = dot(grads, down_parts[0], COL_COL)
    back_rest = dot(grads, jnp.concatenate(down_parts[1:], axis=0), COL_COL, BF16)

    def message(d):
        part = back_own.astype(BF16) if d == 0 else back_rest[:, (d % size - 1) * share : d % size * share]
        return jnp.concatenate([hidden, part], axis=0)

    came = swap(message)
    hidden_all = jnp.concatenate([part[:capacity] for part in came], axis=1)
    back = add(back_own, *(part[capacity:] for part in came[1:]))
    out = dot(hidden_all, down, ROW_COL)
    mixed = assemble(collect(carry((weight * out).astype(BF16))), pool_order, BF16)

    hidden_grad = weight * back
    gate_back = (hidden_grad * up_pre * (sig * (1.0 + gate_pre * (1.0 - sig)))).astype(BF16)
    up_back = (hidden_grad * act).astype(BF16)

    def share_in(d):
        return dot(gate_back, rows(wg, cols)(d), COL_COL) + dot(up_back, rows(wu, cols)(d), COL_COL)

    grad_block, hops = ring_sum(share_in)
    grad_block = grad_block.astype(BF16)
    got = carry(grad_block)

    gate_sum = jnp.sum(grads.astype(F32) * out, axis=1)[None, :]
    gate_rows = jnp.concatenate(thirds(gate_sum), axis=0)
    gate_rows = jnp.pad(gate_rows, ((0, 13), (0, cols - capacity)))
    scaled = (weight * after(hidden_all, *hops).astype(F32)).astype(BF16)
    down_grad = dot(scaled, grads, ROW_ROW, BF16)
    down_grad = swap(
        lambda d: jnp.concatenate([down_grad[d % size * share : (d % size + 1) * share], gate_rows], axis=0)
    )
    gate_parts = [part[share : share + 3, :capacity].astype(F32) for part in down_grad]
    gate_parts = [part[0:1] + part[1:2] + part[2:3] for part in gate_parts]
    gate_grad = (gate_parts[0] + gate_parts[2]) + (gate_parts[1] + gate_parts[3])
    wd_grad = assemble([part[:share] for part in down_grad], pool_order, F32)
    wg_grad, wu_grad = weight_grads(
        inputs, pool_order, after(gate_back, grad_block), after(up_back, grad_block)
    )
    got = after(got, mixed, wd_grad, wg_grad, wu_grad, gate_grad)
    token_grad = assemble(collect(got), pool_order, BF16)
    return (mixed, token_grad, gate_grad, wg_grad[None], wu_grad[None], wd_grad[None])


def solution(mesh):
    return jax.shard_map(
        body,
        mesh=mesh,
        in_specs=(
            P(BOTH, None),
            P(BOTH),
            P(),
            P("ep", None),
            P("ep", None, "pool"),
            P("ep", None, "pool"),
            P("ep", "pool", None),
            P(BOTH, None),
        ),
        out_specs=(
            P(BOTH, None),
            P(BOTH, None),
            P("ep", None),
            P("ep", None, "pool"),
            P("ep", None, "pool"),
            P("ep", "pool", None),
        ),
        check_vma=False,
    )
```

```python
import jax
import jax.numpy as jnp
from jax import lax
from jax.experimental import pallas as pl
from jax.experimental.pallas import tpu as pltpu
from jax.sharding import PartitionSpec as P

BF16 = jnp.bfloat16
F32 = jnp.float32
BOTH = ("pool", "ep")
ROW_COL = ((1,), (0,))
COL_COL = ((1,), (1,))
ROW_ROW = ((0,), (0,))


def dot(a, b, dims, out=F32):
    return lax.dot_general(a, b, (dims, ((), ())), preferred_element_type=out)


def add(*terms):
    total = terms[0].astype(F32)
    for term in terms[1:]:
        total = total + term.astype(F32)
    return total


def shift(value, step):
    size = lax.axis_size("pool")
    return lax.ppermute(value, "pool", [(i, (i + step) % size) for i in range(size)])


def after(value, *earlier):
    return lax.optimization_barrier((value, *earlier))[0]


def swap(get):
    behind = shift(get(-1), -1)
    before = shift(get(1), 1)
    far = shift(get(2), 2)
    return [get(0), behind, far, before]


def ring_gather(block):
    half = block.shape[0] // 2
    before, behind = shift(block, 1), shift(block, -1)
    far = (shift(before[:half], 1), shift(behind[half:], -1))
    block, behind, before = ((piece[:half], piece[half:]) for piece in (block, behind, before))
    return [block, behind, far, before]


def thirds(value):
    high = lax.optimization_barrier(value.astype(BF16))
    rest = value - high.astype(F32)
    middle = lax.optimization_barrier(rest.astype(BF16))
    return high, middle, (rest - middle.astype(F32)).astype(BF16)


def kept(shape, dtype):
    return pltpu.HBM(shape, dtype)


def from_hbm(*arrays):
    return [pltpu.with_memory_space_constraint(array, pltpu.HBM) for array in arrays]


def whole_block(shape):
    return pl.BlockSpec(shape, lambda *index: (0,) * len(shape))


def params(megabytes):
    return pltpu.CompilerParams(vmem_limit_bytes=megabytes * 1024 * 1024)


def cost(flops, arrays):
    size = sum(int(array.size) * jnp.dtype(array.dtype).itemsize for array in arrays)
    return pl.CostEstimate(flops=int(flops), bytes_accessed=size, transcendentals=0)


def masked_send(pick, parts, text_rows):
    total, held = pick.shape
    rows = held // len(parts)
    cols = parts[0].shape[1]
    tile = total // 4

    def kernel(pick_ref, *refs):
        part_refs, out_ref, values, kinds = refs[: len(parts)], refs[-3], refs[-2], refs[-1]
        step = pl.program_id(0)

        @pl.when(step == 0)
        def _():
            for d, ref in enumerate(part_refs):
                values[d * rows : (d + 1) * rows, :] = ref[:rows, :]
                kinds[:, d * rows : (d + 1) * rows] = ref[rows:, :rows]

        kind = kinds[:1, :].astype(F32)
        row = step * tile + lax.broadcasted_iota(jnp.int32, (tile, 1), 0)
        keep = jnp.where(row < text_rows, 1.0 - kind, kind)
        chosen = (pick_ref[...].astype(F32) * keep).astype(BF16)
        out_ref[...] = dot(chosen, values[...], ROW_COL).astype(BF16)

    return pl.pallas_call(
        kernel,
        grid=(4,),
        out_shape=kept((total, cols), BF16),
        in_specs=[pl.BlockSpec((tile, held), lambda i: (i, 0))]
        + [pl.BlockSpec(part.shape, lambda i: (0, 0)) for part in parts],
        out_specs=pl.BlockSpec((tile, cols), lambda i: (i, 0)),
        scratch_shapes=[pltpu.VMEM((held, cols), BF16), pltpu.VMEM((16, held), BF16)],
        cost_estimate=pl.CostEstimate(
            flops=2 * total * held * cols, bytes_accessed=2 * (total * cols * 2 + total * held), transcendentals=0
        ),
        compiler_params=params(8),
    )(pick, *parts)


def assemble(parts, members, dtype, rows):
    cols = parts[0].shape[1]

    def kernel(members_ref, *refs):
        for d, ref in enumerate(refs[:-1]):

            @pl.when(pl.program_id(0) == d)
            def _(ref=ref):
                refs[-1][...] = ref[...].astype(dtype)

    return pl.pallas_call(
        kernel,
        grid_spec=pltpu.PrefetchScalarGridSpec(
            num_scalar_prefetch=1,
            grid=(len(parts),),
            in_specs=[pl.BlockSpec((rows, cols), lambda d, m: (0, 0)) for _ in parts],
            out_specs=pl.BlockSpec((rows, cols), lambda d, m: (0, m[d])),
        ),
        out_shape=jax.ShapeDtypeStruct((rows, len(parts) * cols), dtype),
        cost_estimate=pl.CostEstimate(
            flops=0, bytes_accessed=len(parts) * rows * cols * (2 + jnp.dtype(dtype).itemsize), transcendentals=0
        ),
        compiler_params=params(10),
    )(members, *parts)


def weight_grads(inputs, members, gate_back, up_back):
    half, cols = inputs[0][0].shape
    share = gate_back.shape[1]

    def kernel(members_ref, *refs):
        gate_ref, up_ref, gate_out, up_out = refs[-4:]
        for d in range(len(inputs)):

            @pl.when(pl.program_id(0) == d)
            def _(top=refs[2 * d], low=refs[2 * d + 1]):
                for grad, out in ((gate_ref, gate_out), (up_ref, up_out)):
                    out[...] = dot(top[...], grad[:half, :], ROW_ROW) + dot(low[...], grad[half:, :], ROW_ROW)

    whole = jax.ShapeDtypeStruct((len(inputs) * cols, share), F32)
    return pl.pallas_call(
        kernel,
        grid_spec=pltpu.PrefetchScalarGridSpec(
            num_scalar_prefetch=1,
            grid=(len(inputs),),
            in_specs=[pl.BlockSpec((half, cols), lambda d, m: (0, 0)) for _ in inputs for _ in range(2)]
            + [pl.BlockSpec((2 * half, share), lambda d, m: (0, 0))] * 2,
            out_specs=[pl.BlockSpec((cols, share), lambda d, m: (m[d], 0))] * 2,
        ),
        out_shape=[whole, whole],
        cost_estimate=pl.CostEstimate(
            flops=8 * half * cols * share * len(inputs),
            bytes_accessed=len(inputs) * (half * cols * 4 + cols * share * 8),
            transcendentals=0,
        ),
        compiler_params=params(14),
    )(members, *[piece for pair in inputs for piece in pair], gate_back, up_back)


def hidden_from(gate_sum, up_sum, far, w_gate, w_up, members):
    half, cols = far[0].shape
    count, share = gate_sum.shape

    def kernel(members_ref, gate_ref, up_ref, top, low, wg_ref, wu_ref, gate_out, up_out, hidden_out):
        for start, ref in ((0, top), (half, low)):
            span = slice(start, start + half)
            gate = gate_ref[span, :] + dot(ref[...], wg_ref[...], ROW_COL)
            up = up_ref[span, :] + dot(ref[...], wu_ref[...], ROW_COL)
            gate_out[span, :] = gate
            up_out[span, :] = up
            hidden_out[span, :] = (gate * jax.nn.sigmoid(gate) * up).astype(BF16)

    wide = kept((count, share), F32)
    return pl.pallas_call(
        kernel,
        grid_spec=pltpu.PrefetchScalarGridSpec(
            num_scalar_prefetch=1,
            grid=(1,),
            in_specs=[whole_block((count, share))] * 2
            + [whole_block((half, cols))] * 2
            + [pl.BlockSpec((cols, share), lambda i, m: (m[2], 0))] * 2,
            out_specs=[whole_block((count, share))] * 3,
        ),
        out_shape=[wide, wide, jax.ShapeDtypeStruct((count, share), BF16)],
        cost_estimate=cost(4 * count * cols * share, (gate_sum, up_sum, *far, gate_sum, up_sum)),
        compiler_params=params(8),
    )(members, gate_sum, up_sum, *far, w_gate, w_up)


def fetch_and_back(place_in, got, down_parts):
    count, total = place_in.shape
    share, cols = down_parts[0].shape
    tile = count // 2

    def kernel(place_ref, got_ref, *refs):
        downs, (rows_out, *back_out) = refs[: len(down_parts)], refs[len(down_parts) :]
        rows = dot(place_ref[...], got_ref[...], ROW_COL).astype(BF16)
        rows_out[...] = rows
        for down, out in zip(downs, back_out):
            out[...] = dot(rows, down[...], COL_COL).astype(out.dtype)

    kinds = [F32] + [BF16] * (len(down_parts) - 1)
    return pl.pallas_call(
        kernel,
        grid=(2,),
        in_specs=[pl.BlockSpec((tile, total), lambda i: (i, 0)), whole_block(got.shape)]
        + [whole_block((share, cols))] * len(down_parts),
        out_specs=[pl.BlockSpec((tile, cols), lambda i: (i, 0))]
        + [pl.BlockSpec((tile, share), lambda i: (i, 0))] * len(kinds),
        out_shape=[kept((count, cols), BF16)]
        + [jax.ShapeDtypeStruct((count, share), kind) for kind in kinds],
        cost_estimate=cost(2 * count * total * cols + 8 * count * share * cols, (place_in, got, *down_parts)),
        compiler_params=params(14),
    )(*from_hbm(place_in, got, *down_parts))


def weighted_slots(hidden_parts, down_parts, weight, grads, place_out):
    total, count = place_out.shape
    share, cols = down_parts[0].shape
    tile = cols // 4
    pieces = len(hidden_parts)

    def kernel(*refs):
        hiddens, downs = refs[:pieces], refs[pieces : 2 * pieces]
        weight_ref, grads_ref, place_ref, slots_out, gate_out = refs[2 * pieces :]
        hidden = jnp.concatenate([ref[...] for ref in hiddens], axis=1)
        out = dot(hidden, jnp.concatenate([ref[...] for ref in downs], axis=0), ROW_COL)
        slots_out[...] = dot(place_ref[...], (weight_ref[...] * out).astype(BF16), ROW_COL).astype(BF16)
        gate = jnp.sum(grads_ref[...].astype(F32) * out, axis=1, keepdims=True)

        @pl.when(pl.program_id(0) == 0)
        def _():
            gate_out[...] = gate

        @pl.when(pl.program_id(0) > 0)
        def _():
            gate_out[...] += gate

    return pl.pallas_call(
        kernel,
        grid=(4,),
        in_specs=[whole_block((count, share))] * pieces
        + [pl.BlockSpec((share, tile), lambda i: (0, i))] * pieces
        + [whole_block((count, 1)), pl.BlockSpec((count, tile), lambda i: (0, i)), whole_block((total, count))],
        out_specs=[pl.BlockSpec((total, tile), lambda i: (0, i)), whole_block((count, 1))],
        out_shape=[kept((total, cols), BF16), kept((count, 1), F32)],
        cost_estimate=cost(
            2 * count * cols * (total + pieces * share), (*hidden_parts, *down_parts, grads, place_out, place_out)
        ),
        compiler_params=params(10),
    )(*hidden_parts, *down_parts, weight, grads, place_out)


def first_hop(back_parts, gate_pre, up_pre, weight, w_gate, w_up, order):
    count, share = gate_pre.shape
    half = count // 2
    cols = w_gate.shape[0] // (len(order) + 1)
    pieces = len(back_parts)

    def kernel(order_ref, *refs):
        gate_ref, up_ref, weight_ref, wg_ref, wu_ref = refs[pieces : pieces + 5]
        gate_out, up_out, rise_out, fall_out = refs[pieces + 5 :]
        step = pl.program_id(0)

        @pl.when(step == 0)
        def _():
            back = weight_ref[...] * add(*(ref[...] for ref in refs[:pieces]))
            gate = gate_ref[...]
            sig = jax.nn.sigmoid(gate)
            gate_out[...] = (back * up_ref[...] * (sig * (1.0 + gate * (1.0 - sig)))).astype(BF16)
            up_out[...] = (back * (gate * sig)).astype(BF16)

        def product(start, stop):
            grads = jnp.concatenate([gate_out[start:stop, :], up_out[start:stop, :]], axis=1)
            weights = jnp.concatenate([wg_ref[...], wu_ref[...]], axis=1)
            return dot(grads, weights, COL_COL).astype(BF16)

        @pl.when(step == 0)
        def _():
            rows = product(0, count)
            rise_out[:half, :] = rows[:half]
            fall_out[half:, :] = rows[half:]

        @pl.when(step == 1)
        def _():
            rise_out[half:, :] = product(half, count)

        @pl.when(step == 2)
        def _():
            fall_out[:half, :] = product(0, half)

    small = kept((count, share), BF16)
    wide = kept((count, cols), BF16)
    return pl.pallas_call(
        kernel,
        grid_spec=pltpu.PrefetchScalarGridSpec(
            num_scalar_prefetch=1,
            grid=(len(order),),
            in_specs=[whole_block((count, share))] * (pieces + 2)
            + [whole_block((count, 1))]
            + [pl.BlockSpec((cols, share), lambda j, m: (m[j], 0))] * 2,
            out_specs=[whole_block((count, share))] * 2
            + [whole_block((count, cols))] * 2,
        ),
        out_shape=[small, small, wide, wide],
        cost_estimate=cost(8 * count * share * cols, (*back_parts, gate_pre, up_pre, w_gate, w_up)),
        compiler_params=params(16),
    )(jnp.stack(order).astype(jnp.int32), *back_parts, *from_hbm(gate_pre, up_pre, weight, w_gate, w_up))


def summed_slots(own, rise, fall, rise_last, fall_last, place_out):
    total, count = place_out.shape
    half, cols = rise_last.shape
    tile = cols // 4

    def kernel(own_ref, rise_ref, fall_ref, rise_last_ref, fall_last_ref, place_ref, out_ref):
        top = add(own_ref[:half, :], rise_last_ref[...], fall_ref[...])
        low = add(own_ref[half:, :], rise_ref[...], fall_last_ref[...])
        sums = jnp.concatenate([top, low], axis=0).astype(BF16)
        out_ref[...] = dot(place_ref[...], sums, ROW_COL).astype(BF16)

    return pl.pallas_call(
        kernel,
        grid=(4,),
        in_specs=[
            pl.BlockSpec((count, tile), lambda i: (0, i)),
            pl.BlockSpec((half, tile), lambda i: (1, i)),
            pl.BlockSpec((half, tile), lambda i: (0, i)),
            pl.BlockSpec((half, tile), lambda i: (0, i)),
            pl.BlockSpec((half, tile), lambda i: (0, i)),
            whole_block((total, count)),
        ],
        out_specs=pl.BlockSpec((total, tile), lambda i: (0, i)),
        out_shape=kept((total, cols), BF16),
        cost_estimate=cost(2 * total * count * cols, (own, rise, fall, place_out, place_out)),
        compiler_params=params(10),
    )(own, rise, fall, rise_last, fall_last, place_out)


def body(tokens, modality, chosen, gates, w_gate, w_up, w_down, cotangent):
    tok_rows, width = tokens.shape
    size = lax.axis_size("pool")
    ep_size = lax.axis_size("ep")
    slots = 2 * tok_rows // ep_size
    capacity = chosen.shape[1]
    text_count = 3 * ep_size // 4
    cols = width // size
    share = w_gate.shape[2]
    me = lax.axis_index("pool")
    mine = lax.axis_index("ep")
    members = [(me + d) % size for d in range(size)]
    pool_order = jnp.stack(members).astype(jnp.int32)

    def columns(array):
        return lambda d: lax.dynamic_slice(
            array, (0, members[d % size] * cols), (array.shape[0], cols)
        )

    def rows(array, count):
        return lambda d: lax.dynamic_slice(
            array, (members[d % size] * count, 0), (count, array.shape[1])
        )

    extra = jnp.broadcast_to(jnp.pad(modality, (0, cols - tok_rows)).astype(BF16), (16, cols))
    token_parts = swap(lambda d: jnp.concatenate([columns(tokens)(d), extra], axis=0))
    later = token_parts[1:]
    grad_parts = swap(lambda d: after(columns(cotangent)(d), *later) if d == 2 else columns(cotangent)(d))
    down_parts = swap(lambda d: after(columns(w_down[0])(d), *later))

    token_at = []
    for d in range(size):
        first = (members[d] * ep_size + mine) * tok_rows
        local = chosen - first
        below = jnp.sum((local < 0).astype(jnp.int32), axis=1, keepdims=True)
        inside = (local >= 0) & (local < tok_rows)
        place = jnp.where(inside, jnp.arange(capacity, dtype=jnp.int32)[None, :] - below, -1)
        at_slot = place[:, None, :] == jnp.arange(slots, dtype=jnp.int32)[None, :, None]
        held = jnp.sum(jnp.where(at_slot, local[:, None, :] + 1, 0), axis=2) - 1
        token_at.append(jnp.where(held < 0, -1, held + d * tok_rows))
    token_at = jnp.stack(token_at, axis=1).reshape(ep_size * size * slots, 1)
    token_ids = jnp.arange(size * tok_rows, dtype=jnp.int32)
    pick = (token_at == token_ids[None, :]).astype(BF16)
    pick_back = (token_at.reshape(1, -1) == token_ids[:, None]).astype(BF16)
    pick, pick_back = lax.optimization_barrier((pick, pick_back))

    picks = lax.dynamic_slice_in_dim(chosen, mine, 1, 0)[0]
    holder = picks // tok_rows
    order = jnp.arange(capacity, dtype=jnp.int32)
    same = (holder[:, None] == holder[None, :]) & (order[None, :] < order[:, None])
    rank = jnp.sum(same.astype(jnp.int32), axis=1)
    pool_of, ep_of = holder // ep_size, holder % ep_size
    flat = (ep_of * size + (pool_of - me) % size) * slots + rank
    slot_total = ep_size * size * slots
    slot_ids = jnp.arange(slot_total, dtype=jnp.int32)
    place_in = (flat[:, None] == slot_ids[None, :]).astype(BF16)
    place_out = (flat[None, :] == slot_ids[:, None]).astype(BF16)
    place_in, place_out = lax.optimization_barrier((place_in, place_out))

    def exchange(values):
        blocks = values.reshape(ep_size, size * slots, cols)
        blocks = lax.all_to_all(blocks, "ep", split_axis=0, concat_axis=0, tiled=True)
        return blocks.reshape(slot_total, cols)

    def fetch(got):
        return dot(place_in, got, ROW_COL, BF16)

    def collect(got):
        return dot(pick_back, got, ROW_COL, BF16)

    def return_to_holders(summed):
        parts = swap(lambda d: summed[d % size * tok_rows : (d % size + 1) * tok_rows])
        return assemble(parts, pool_order, BF16, tok_rows)

    wg, wu = w_gate[0], w_up[0]
    weight = gates[0][:, None]
    sent = masked_send(pick, token_parts, text_count * size * slots)
    sent_grads = dot(pick, jnp.concatenate(grad_parts, axis=0), ROW_COL, BF16)
    block = fetch(after(exchange(after(sent, grad_parts[1], grad_parts[3])), sent_grads))
    inputs = ring_gather(block)
    got = exchange(after(sent_grads, block, *down_parts))

    def near_sum(weights):
        halves = [sum(dot(inputs[d][i], rows(weights, cols)(d), ROW_COL) for d in (0, 1, 3)) for i in range(2)]
        return jnp.concatenate(halves, axis=0)

    gate_pre, up_pre, hidden = hidden_from(near_sum(wg), near_sum(wu), inputs[2], wg, wu, pool_order)
    grads, *back_parts = fetch_and_back(place_in, got, down_parts)
    came = swap(lambda d: back_parts[d % size])
    hidden_parts = swap(lambda d: hidden)
    hidden_parts = lax.optimization_barrier((*hidden_parts, *back_parts))[:size]

    slots_out, gate_sum = weighted_slots(hidden_parts, down_parts, weight, grads, place_out)
    came[1] = after(came[1], slots_out)

    gate_back, up_back, rise, fall = first_hop(
        came, gate_pre, up_pre, weight, wg, wu, [members[2], members[1], members[3]]
    )
    sent_first = rise, fall
    mixed_sum = collect(exchange(after(slots_out, *sent_first)))
    mixed = return_to_holders(mixed_sum)
    rise, fall = shift(rise, 1), shift(fall, -1)
    half = capacity // 2

    def share_in(d, span):
        gate, up = (after(grad, *sent_first)[span] for grad in (gate_back, up_back))
        return dot(gate, rows(wg, cols)(d), COL_COL) + dot(up, rows(wu, cols)(d), COL_COL)

    own = share_in(0, slice(None))
    hops = (
        (share_in(1, slice(0, half)) + rise[:half].astype(F32)).astype(BF16),
        (share_in(3, slice(half, None)) + fall[half:].astype(F32)).astype(BF16),
    )
    slots_in = summed_slots(own, rise, fall, shift(hops[0], 1), shift(hops[1], -1), place_out)
    got = exchange(slots_in)

    gate_sum = after(gate_sum, *hops).reshape(1, capacity)
    gate_rows = jnp.concatenate(thirds(gate_sum), axis=0)
    gate_rows = jnp.pad(gate_rows, ((0, 13), (0, cols - capacity)))
    hidden_all = jnp.concatenate(after(hidden_parts, *hops), axis=1)
    scaled = (weight * hidden_all.astype(F32)).astype(BF16)
    down_grad = dot(scaled, grads, ROW_ROW, BF16)
    down_grad = swap(
        lambda d: jnp.concatenate([down_grad[d % size * share : (d % size + 1) * share], gate_rows], axis=0)
    )
    down_grad = [after(part, mixed_sum) for part in down_grad]
    gate_parts = [part[share : share + 3, :capacity].astype(F32) for part in down_grad]
    gate_parts = [part[0:1] + part[1:2] + part[2:3] for part in gate_parts]
    gate_grad = (gate_parts[0] + gate_parts[2]) + (gate_parts[1] + gate_parts[3])
    wd_grad = assemble(down_grad, pool_order, F32, share)
    wg_grad, wu_grad = weight_grads(
        inputs, pool_order, after(gate_back, slots_in, mixed_sum), after(up_back, slots_in)
    )
    got = after(got, mixed, wd_grad, wg_grad, wu_grad, gate_grad)
    token_grad = return_to_holders(collect(got))
    return (mixed, token_grad, gate_grad, wg_grad[None], wu_grad[None], wd_grad[None])


def solution(mesh):
    return jax.shard_map(
        body,
        mesh=mesh,
        in_specs=(
            P(BOTH, None),
            P(BOTH),
            P(),
            P("ep", None),
            P("ep", None, "pool"),
            P("ep", None, "pool"),
            P("ep", "pool", None),
            P(BOTH, None),
        ),
        out_specs=(
            P(BOTH, None),
            P(BOTH, None),
            P("ep", None),
            P("ep", None, "pool"),
            P("ep", None, "pool"),
            P("ep", "pool", None),
        ),
        check_vma=False,
    )
```

```python
import jax
import jax.numpy as jnp
from jax import lax
from jax.experimental import pallas as pl
from jax.experimental.pallas import tpu as pltpu
from jax.sharding import PartitionSpec as P

BF16 = jnp.bfloat16
F32 = jnp.float32
BOTH = ("pool", "ep")
ROW_COL = ((1,), (0,))
COL_COL = ((1,), (1,))
ROW_ROW = ((0,), (0,))


def dot(a, b, dims, out=F32):
    return lax.dot_general(a, b, (dims, ((), ())), preferred_element_type=out)


def add(*terms):
    total = terms[0].astype(F32)
    for term in terms[1:]:
        total = total + term.astype(F32)
    return total


def shift(value, step):
    size = lax.axis_size("pool")
    return lax.ppermute(value, "pool", [(i, (i + step) % size) for i in range(size)])


def after(value, *earlier):
    return lax.optimization_barrier((value, *earlier))[0]


def swap(get):
    behind = shift(get(-1), -1)
    before = shift(get(1), 1)
    far = shift(get(2), 2)
    return [get(0), behind, far, before]


def ring_gather(block):
    half = block.shape[0] // 2
    before, behind = shift(block, 1), shift(block, -1)
    far = shift(before[:half], 1), shift(behind[half:], -1)
    return [block, behind, far, before]


def thirds(value):
    high = lax.optimization_barrier(value.astype(BF16))
    rest = value - high.astype(F32)
    middle = lax.optimization_barrier(rest.astype(BF16))
    return high, middle, (rest - middle.astype(F32)).astype(BF16)


def kept(shape, dtype):
    return pltpu.HBM(shape, dtype)


def from_hbm(*arrays):
    return [pltpu.with_memory_space_constraint(array, pltpu.HBM) for array in arrays]


def whole_block(shape):
    return pl.BlockSpec(shape, lambda *index: (0,) * len(shape))


def params(megabytes):
    return pltpu.CompilerParams(vmem_limit_bytes=megabytes * 1024 * 1024)


def cost(flops, arrays):
    size = sum(int(array.size) * jnp.dtype(array.dtype).itemsize for array in arrays)
    return pl.CostEstimate(flops=int(flops), bytes_accessed=size, transcendentals=0)


def masked_send(pick, parts, text_rows):
    total, held = pick.shape
    rows = held // len(parts)
    cols = parts[0].shape[1]
    tile = total // 4

    def kernel(pick_ref, *refs):
        part_refs, out_ref, values, kinds = refs[: len(parts)], refs[-3], refs[-2], refs[-1]
        step = pl.program_id(0)

        @pl.when(step == 0)
        def _():
            for d, ref in enumerate(part_refs):
                values[d * rows : (d + 1) * rows, :] = ref[:rows, :]
                kinds[:, d * rows : (d + 1) * rows] = ref[rows:, :rows]

        kind = kinds[:1, :].astype(F32)
        row = step * tile + lax.broadcasted_iota(jnp.int32, (tile, 1), 0)
        keep = jnp.where(row < text_rows, 1.0 - kind, kind)
        chosen = (pick_ref[...].astype(F32) * keep).astype(BF16)
        out_ref[...] = dot(chosen, values[...], ROW_COL).astype(BF16)

    return pl.pallas_call(
        kernel,
        grid=(4,),
        out_shape=kept((total, cols), BF16),
        in_specs=[pl.BlockSpec((tile, held), lambda i: (i, 0))]
        + [pl.BlockSpec(part.shape, lambda i: (0, 0)) for part in parts],
        out_specs=pl.BlockSpec((tile, cols), lambda i: (i, 0)),
        scratch_shapes=[pltpu.VMEM((held, cols), BF16), pltpu.VMEM((16, held), BF16)],
        cost_estimate=pl.CostEstimate(
            flops=2 * total * held * cols, bytes_accessed=2 * (total * cols * 2 + total * held), transcendentals=0
        ),
        compiler_params=params(8),
    )(pick, *parts)


def assemble(parts, members, dtype, rows):
    cols = parts[0].shape[1]

    def kernel(members_ref, *refs):
        for d, ref in enumerate(refs[:-1]):
            start = pl.multiple_of(members_ref[d] * cols, 128)
            refs[-1][:, pl.ds(start, cols)] = ref[...].astype(dtype)

    return pl.pallas_call(
        kernel,
        grid_spec=pltpu.PrefetchScalarGridSpec(
            num_scalar_prefetch=1,
            grid=(2,),
            in_specs=[pl.BlockSpec((rows // 2, cols), lambda i, m: (i, 0)) for _ in parts],
            out_specs=pl.BlockSpec((rows // 2, len(parts) * cols), lambda i, m: (i, 0)),
        ),
        out_shape=jax.ShapeDtypeStruct((rows, len(parts) * cols), dtype),
        cost_estimate=pl.CostEstimate(
            flops=0, bytes_accessed=len(parts) * rows * cols * (2 + jnp.dtype(dtype).itemsize), transcendentals=0
        ),
        compiler_params=params(10),
    )(members, *parts)


def weight_grads(inputs, members, gate_back, up_back):
    count, cols = inputs[0].shape
    share = gate_back.shape[1]
    blocks = [block if isinstance(block, tuple) else (block,) for block in inputs]
    pieces = [piece for block in blocks for piece in block]

    def kernel(members_ref, *refs):
        gate_ref, up_ref, gate_out, up_out = refs[-4:]
        refs = list(refs[: len(pieces)])
        for d, block in enumerate(blocks):
            held = [refs.pop(0) for _ in block]

            @pl.when(pl.program_id(0) == d)
            def _(held=held):
                for grad, out in ((gate_ref, gate_out), (up_ref, up_out)):
                    size = held[0].shape[0]
                    out[...] = sum(
                        dot(ref[...], grad[i * size : (i + 1) * size, :], ROW_ROW) for i, ref in enumerate(held)
                    )

    whole = jax.ShapeDtypeStruct((len(inputs) * cols, share), F32)
    return pl.pallas_call(
        kernel,
        grid_spec=pltpu.PrefetchScalarGridSpec(
            num_scalar_prefetch=1,
            grid=(len(inputs),),
            in_specs=[whole_block(piece.shape) for piece in pieces] + [whole_block((count, share))] * 2,
            out_specs=[pl.BlockSpec((cols, share), lambda d, m: (m[d], 0))] * 2,
        ),
        out_shape=[whole, whole],
        cost_estimate=pl.CostEstimate(
            flops=4 * count * cols * share * len(inputs),
            bytes_accessed=len(inputs) * (count * cols * 2 + cols * share * 8),
            transcendentals=0,
        ),
        compiler_params=params(16),
    )(members, *pieces, gate_back, up_back)


def hidden_from(gate_sum, up_sum, far, w_gate, w_up, members):
    half, cols = far[0].shape
    count, share = gate_sum.shape

    def kernel(members_ref, gate_ref, up_ref, top, low, wg_ref, wu_ref, gate_out, up_out, hidden_out):
        for start, ref in ((0, top), (half, low)):
            span = slice(start, start + half)
            gate = gate_ref[span, :] + dot(ref[...], wg_ref[...], ROW_COL)
            up = up_ref[span, :] + dot(ref[...], wu_ref[...], ROW_COL)
            gate_out[span, :] = gate
            up_out[span, :] = up
            hidden_out[span, :] = (gate * jax.nn.sigmoid(gate) * up).astype(BF16)

    wide = kept((count, share), F32)
    return pl.pallas_call(
        kernel,
        grid_spec=pltpu.PrefetchScalarGridSpec(
            num_scalar_prefetch=1,
            grid=(1,),
            in_specs=[whole_block((count, share))] * 2
            + [whole_block((half, cols))] * 2
            + [pl.BlockSpec((cols, share), lambda i, m: (m[2], 0))] * 2,
            out_specs=[whole_block((count, share))] * 3,
        ),
        out_shape=[wide, wide, jax.ShapeDtypeStruct((count, share), BF16)],
        cost_estimate=cost(4 * count * cols * share, (gate_sum, up_sum, *far, gate_sum, up_sum)),
        compiler_params=params(8),
    )(members, gate_sum, up_sum, *far, w_gate, w_up)


def fetch_and_back(place_in, got, down_parts):
    count, total = place_in.shape
    share, cols = down_parts[0].shape
    tile = count // 2

    def kernel(place_ref, got_ref, *refs):
        downs, (rows_out, *back_out) = refs[: len(down_parts)], refs[len(down_parts) :]
        rows = dot(place_ref[...], got_ref[...], ROW_COL).astype(BF16)
        rows_out[...] = rows
        for down, out in zip(downs, back_out):
            out[...] = dot(rows, down[...], COL_COL).astype(out.dtype)

    kinds = [F32] + [BF16] * (len(down_parts) - 1)
    return pl.pallas_call(
        kernel,
        grid=(2,),
        in_specs=[pl.BlockSpec((tile, total), lambda i: (i, 0)), whole_block(got.shape)]
        + [whole_block((share, cols))] * len(down_parts),
        out_specs=[pl.BlockSpec((tile, cols), lambda i: (i, 0))]
        + [pl.BlockSpec((tile, share), lambda i: (i, 0))] * len(kinds),
        out_shape=[kept((count, cols), BF16)]
        + [jax.ShapeDtypeStruct((count, share), kind) for kind in kinds],
        cost_estimate=cost(2 * count * total * cols + 8 * count * share * cols, (place_in, got, *down_parts)),
        compiler_params=params(14),
    )(*from_hbm(place_in, got, *down_parts))


def weighted_slots(hidden_parts, down_parts, weight, place_out):
    total, count = place_out.shape
    share, cols = down_parts[0].shape
    tile = cols // 4
    pieces = len(hidden_parts)

    def kernel(*refs):
        hiddens, downs = refs[:pieces], refs[pieces : 2 * pieces]
        weight_ref, place_ref, slots_out = refs[2 * pieces :]
        hidden = jnp.concatenate([ref[...] for ref in hiddens], axis=1)
        out = dot(hidden, jnp.concatenate([ref[...] for ref in downs], axis=0), ROW_COL)
        slots_out[...] = dot(place_ref[...], (weight_ref[...] * out).astype(BF16), ROW_COL).astype(BF16)

    return pl.pallas_call(
        kernel,
        grid=(4,),
        in_specs=[whole_block((count, share))] * pieces
        + [pl.BlockSpec((share, tile), lambda i: (0, i))] * pieces
        + [whole_block((count, 1)), whole_block((total, count))],
        out_specs=pl.BlockSpec((total, tile), lambda i: (0, i)),
        out_shape=kept((total, cols), BF16),
        cost_estimate=cost(
            2 * count * cols * (total + pieces * share), (*hidden_parts, *down_parts, place_out, place_out)
        ),
        compiler_params=params(10),
    )(*hidden_parts, *down_parts, weight, place_out)


def first_hop(back_parts, hidden, gate_pre, up_pre, weight, w_gate, w_up, order):
    count, share = gate_pre.shape
    half = count // 2
    cols = w_gate.shape[0] // (len(order) + 1)
    pieces = len(back_parts)

    def kernel(order_ref, *refs):
        hidden_ref, gate_ref, up_ref, weight_ref, wg_ref, wu_ref = refs[pieces : pieces + 6]
        gate_out, up_out, rise_out, fall_out, sum_out = refs[pieces + 6 :]
        step = pl.program_id(0)

        @pl.when(step == 0)
        def _():
            back = add(*(ref[...] for ref in refs[:pieces]))
            sum_out[...] = jnp.sum(hidden_ref[...].astype(F32) * back, axis=1, keepdims=True)
            back = weight_ref[...] * back
            gate = gate_ref[...]
            sig = jax.nn.sigmoid(gate)
            gate_out[...] = (back * up_ref[...] * (sig * (1.0 + gate * (1.0 - sig)))).astype(BF16)
            up_out[...] = (back * (gate * sig)).astype(BF16)

        def product(start, stop):
            grads = jnp.concatenate([gate_out[start:stop, :], up_out[start:stop, :]], axis=1)
            weights = jnp.concatenate([wg_ref[...], wu_ref[...]], axis=1)
            return dot(grads, weights, COL_COL).astype(BF16)

        @pl.when(step == 0)
        def _():
            rows = product(0, count)
            rise_out[:half, :] = rows[:half]
            fall_out[half:, :] = rows[half:]

        @pl.when(step == 1)
        def _():
            rise_out[half:, :] = product(half, count)

        @pl.when(step == 2)
        def _():
            fall_out[:half, :] = product(0, half)

    small = kept((count, share), BF16)
    wide = kept((count, cols), BF16)
    return pl.pallas_call(
        kernel,
        grid_spec=pltpu.PrefetchScalarGridSpec(
            num_scalar_prefetch=1,
            grid=(len(order),),
            in_specs=[whole_block((count, share))] * (pieces + 3)
            + [whole_block((count, 1))]
            + [pl.BlockSpec((cols, share), lambda j, m: (m[j], 0))] * 2,
            out_specs=[whole_block((count, share))] * 2
            + [whole_block((count, cols))] * 2
            + [whole_block((count, 1))],
        ),
        out_shape=[small, small, wide, wide, kept((count, 1), F32)],
        cost_estimate=cost(8 * count * share * cols, (*back_parts, gate_pre, up_pre, w_gate, w_up)),
        compiler_params=params(16),
    )(jnp.stack(order).astype(jnp.int32), *back_parts, hidden, *from_hbm(gate_pre, up_pre, weight, w_gate, w_up))


def summed_slots(own, rise, fall, rise_last, fall_last, place_out):
    total, count = place_out.shape
    half, cols = rise_last.shape
    tile = cols // 4

    def kernel(own_ref, rise_ref, fall_ref, rise_last_ref, fall_last_ref, place_ref, out_ref):
        top = add(own_ref[:half, :], rise_last_ref[...], fall_ref[...])
        low = add(own_ref[half:, :], rise_ref[...], fall_last_ref[...])
        sums = jnp.concatenate([top, low], axis=0).astype(BF16)
        out_ref[...] = dot(place_ref[...], sums, ROW_COL).astype(BF16)

    return pl.pallas_call(
        kernel,
        grid=(4,),
        in_specs=[
            pl.BlockSpec((count, tile), lambda i: (0, i)),
            pl.BlockSpec((half, tile), lambda i: (1, i)),
            pl.BlockSpec((half, tile), lambda i: (0, i)),
            pl.BlockSpec((half, tile), lambda i: (0, i)),
            pl.BlockSpec((half, tile), lambda i: (0, i)),
            whole_block((total, count)),
        ],
        out_specs=pl.BlockSpec((total, tile), lambda i: (0, i)),
        out_shape=kept((total, cols), BF16),
        cost_estimate=cost(2 * total * count * cols, (own, rise, fall, place_out, place_out)),
        compiler_params=params(10),
    )(own, rise, fall, rise_last, fall_last, place_out)


def body(tokens, modality, chosen, gates, w_gate, w_up, w_down, cotangent):
    tok_rows, width = tokens.shape
    size = lax.axis_size("pool")
    ep_size = lax.axis_size("ep")
    slots = 2 * tok_rows // ep_size
    capacity = chosen.shape[1]
    text_count = 3 * ep_size // 4
    cols = width // size
    share = w_gate.shape[2]
    me = lax.axis_index("pool")
    mine = lax.axis_index("ep")
    members = [(me + d) % size for d in range(size)]
    pool_order = jnp.stack(members).astype(jnp.int32)

    def columns(array):
        return lambda d: lax.dynamic_slice(
            array, (0, members[d % size] * cols), (array.shape[0], cols)
        )

    def rows(array, count):
        return lambda d: lax.dynamic_slice(
            array, (members[d % size] * count, 0), (count, array.shape[1])
        )

    extra = jnp.broadcast_to(jnp.pad(modality, (0, cols - tok_rows)).astype(BF16), (16, cols))
    token_parts = swap(lambda d: jnp.concatenate([columns(tokens)(d), extra], axis=0))
    later = token_parts[1:]
    grad_parts = swap(lambda d: after(columns(cotangent)(d), *later) if d == 2 else columns(cotangent)(d))
    down_parts = swap(lambda d: after(columns(w_down[0])(d), *later))

    token_at = []
    for d in range(size):
        first = (members[d] * ep_size + mine) * tok_rows
        local = chosen - first
        below = jnp.sum((local < 0).astype(jnp.int32), axis=1, keepdims=True)
        inside = (local >= 0) & (local < tok_rows)
        place = jnp.where(inside, jnp.arange(capacity, dtype=jnp.int32)[None, :] - below, -1)
        at_slot = place[:, None, :] == jnp.arange(slots, dtype=jnp.int32)[None, :, None]
        held = jnp.sum(jnp.where(at_slot, local[:, None, :] + 1, 0), axis=2) - 1
        token_at.append(jnp.where(held < 0, -1, held + d * tok_rows))
    token_at = jnp.stack(token_at, axis=1).reshape(ep_size * size * slots, 1)
    token_ids = jnp.arange(size * tok_rows, dtype=jnp.int32)
    pick = (token_at == token_ids[None, :]).astype(BF16)
    pick_back = (token_at.reshape(1, -1) == token_ids[:, None]).astype(BF16)
    pick, pick_back = lax.optimization_barrier((pick, pick_back))

    picks = lax.dynamic_slice_in_dim(chosen, mine, 1, 0)[0]
    holder = picks // tok_rows
    order = jnp.arange(capacity, dtype=jnp.int32)
    same = (holder[:, None] == holder[None, :]) & (order[None, :] < order[:, None])
    rank = jnp.sum(same.astype(jnp.int32), axis=1)
    pool_of, ep_of = holder // ep_size, holder % ep_size
    flat = (ep_of * size + (pool_of - me) % size) * slots + rank
    slot_total = ep_size * size * slots
    slot_ids = jnp.arange(slot_total, dtype=jnp.int32)
    place_in = (flat[:, None] == slot_ids[None, :]).astype(BF16)
    place_out = (flat[None, :] == slot_ids[:, None]).astype(BF16)
    place_in, place_out = lax.optimization_barrier((place_in, place_out))

    def exchange(values):
        blocks = values.reshape(ep_size, size * slots, cols)
        blocks = lax.all_to_all(blocks, "ep", split_axis=0, concat_axis=0, tiled=True)
        return blocks.reshape(slot_total, cols)

    def fetch(got):
        return dot(place_in, got, ROW_COL, BF16)

    def collect(got):
        return dot(pick_back, got, ROW_COL, BF16)

    def of_holder(summed, d):
        return summed[d % size * tok_rows : (d % size + 1) * tok_rows]

    wg, wu = w_gate[0], w_up[0]
    weight = gates[0][:, None]
    sent = masked_send(pick, token_parts, text_count * size * slots)
    sent_grads = dot(pick, jnp.concatenate(grad_parts, axis=0), ROW_COL, BF16)
    block = fetch(after(exchange(after(sent, grad_parts[1], grad_parts[3])), sent_grads))
    inputs = ring_gather(block)
    got = exchange(after(sent_grads, block, *down_parts))

    def near_sum(weights):
        return sum(dot(inputs[d], rows(weights, cols)(d), ROW_COL) for d in (0, 1, 3))

    gate_pre, up_pre, hidden = hidden_from(near_sum(wg), near_sum(wu), inputs[2], wg, wu, pool_order)
    grads, *back_parts = fetch_and_back(place_in, got, down_parts)
    came = swap(lambda d: back_parts[d % size])
    hidden_parts = swap(lambda d: hidden)
    hidden_parts = lax.optimization_barrier((*hidden_parts, *back_parts))[:size]

    slots_out = weighted_slots(hidden_parts, down_parts, weight, place_out)
    came[1] = after(came[1], slots_out)
    gate_back, up_back, rise, fall, gate_sum = first_hop(
        came, hidden, gate_pre, up_pre, weight, wg, wu, [members[2], members[1], members[3]]
    )
    sent_first = rise, fall
    mixed_sum = collect(exchange(after(slots_out, *sent_first)))
    rise, fall = shift(rise, 1), shift(fall, -1)
    half = capacity // 2

    def share_in(d, span):
        gate, up = (after(grad, *sent_first)[span] for grad in (gate_back, up_back))
        return dot(gate, rows(wg, cols)(d), COL_COL) + dot(up, rows(wu, cols)(d), COL_COL)

    own = share_in(0, slice(None))
    hops = (
        (share_in(1, slice(0, half)) + rise[:half].astype(F32)).astype(BF16),
        (share_in(3, slice(half, None)) + fall[half:].astype(F32)).astype(BF16),
    )
    last = shift(hops[0], 1), shift(hops[1], -1)
    slots_in = summed_slots(own, rise, fall, *last, place_out)
    got = exchange(slots_in)

    gate_sum = after(gate_sum, *hops).reshape(1, capacity)
    gate_rows = jnp.concatenate(thirds(gate_sum), axis=0)
    gate_rows = jnp.pad(gate_rows, ((0, 13), (0, cols - capacity)))
    mixed_parts = swap(lambda d: jnp.concatenate([of_holder(mixed_sum, d), gate_rows], axis=0))
    mixed = assemble(mixed_parts, pool_order, BF16, tok_rows)
    gate_parts = [part[tok_rows : tok_rows + 3, :capacity].astype(F32) for part in mixed_parts]
    gate_parts = [part[0:1] + part[1:2] + part[2:3] for part in gate_parts]
    gate_grad = (gate_parts[0] + gate_parts[2]) + (gate_parts[1] + gate_parts[3])
    hidden_all = jnp.concatenate(after(hidden_parts, *hops), axis=1)
    scaled = (weight * hidden_all.astype(F32)).astype(BF16)
    down_grad = dot(scaled, grads, ROW_ROW, BF16)

    def down_block(d):
        block = down_grad[d % size * share : (d % size + 1) * share]
        return after(block, *last) if d == 2 else block

    down_grad = swap(down_block)
    down_grad = [after(part, mixed_sum) for part in down_grad]
    wd_grad = assemble(down_grad, pool_order, F32, share)
    wg_grad, wu_grad = weight_grads(
        inputs, pool_order, after(gate_back, slots_in, mixed_sum), after(up_back, slots_in)
    )
    got = after(got, mixed, wd_grad, wg_grad, wu_grad, gate_grad)
    summed = collect(got)
    token_grad = assemble(swap(lambda d: of_holder(summed, d)), pool_order, BF16, tok_rows)
    return (mixed, token_grad, gate_grad, wg_grad[None], wu_grad[None], wd_grad[None])


def solution(mesh):
    return jax.shard_map(
        body,
        mesh=mesh,
        in_specs=(
            P(BOTH, None),
            P(BOTH),
            P(),
            P("ep", None),
            P("ep", None, "pool"),
            P("ep", None, "pool"),
            P("ep", "pool", None),
            P(BOTH, None),
        ),
        out_specs=(
            P(BOTH, None),
            P(BOTH, None),
            P("ep", None),
            P("ep", None, "pool"),
            P("ep", None, "pool"),
            P("ep", "pool", None),
        ),
        check_vma=False,
    )
```

```python
import jax
import jax.numpy as jnp
from jax import lax
from jax.experimental import pallas as pl
from jax.experimental.pallas import tpu as pltpu
from jax.sharding import PartitionSpec as P

BF16 = jnp.bfloat16
F32 = jnp.float32
BOTH = ("pool", "ep")
ROW_COL = ((1,), (0,))
COL_COL = ((1,), (1,))
ROW_ROW = ((0,), (0,))


def dot(a, b, dims, out=F32):
    return lax.dot_general(a, b, (dims, ((), ())), preferred_element_type=out)


def add(*terms):
    total = terms[0].astype(F32)
    for term in terms[1:]:
        total = total + term.astype(F32)
    return total


def shift(value, step):
    size = lax.axis_size("pool")
    return lax.ppermute(value, "pool", [(i, (i + step) % size) for i in range(size)])


def after(value, *earlier):
    return lax.optimization_barrier((value, *earlier))[0]


def swap(get):
    behind = shift(get(-1), -1)
    before = shift(get(1), 1)
    far = shift(get(2), 2)
    return [get(0), behind, far, before]


def ring_gather(block):
    half = block.shape[0] // 2
    before, behind = shift(block, 1), shift(block, -1)
    far = shift(before[:half], 1), shift(behind[half:], -1)
    return [block, behind, far, before]


def thirds(value):
    high = lax.optimization_barrier(value.astype(BF16))
    rest = value - high.astype(F32)
    middle = lax.optimization_barrier(rest.astype(BF16))
    return high, middle, (rest - middle.astype(F32)).astype(BF16)


def kept(shape, dtype):
    return pltpu.HBM(shape, dtype)


def from_hbm(*arrays):
    return [pltpu.with_memory_space_constraint(array, pltpu.HBM) for array in arrays]


def whole_block(shape):
    return pl.BlockSpec(shape, lambda *index: (0,) * len(shape))


def params(megabytes):
    return pltpu.CompilerParams(vmem_limit_bytes=megabytes * 1024 * 1024)


def cost(flops, arrays):
    size = sum(int(array.size) * jnp.dtype(array.dtype).itemsize for array in arrays)
    return pl.CostEstimate(flops=int(flops), bytes_accessed=size, transcendentals=0)


def token_messages(tokens, modality, members):
    rows, width = tokens.shape
    cols = width // members.shape[0]

    def kernel(members_ref, tokens_ref, modality_ref, *outs):
        for d, out in enumerate(outs):
            start = pl.multiple_of(members_ref[d] * cols, 128)
            out[:rows, :] = tokens_ref[:, pl.ds(start, cols)]
            out[rows:, :] = jnp.zeros((16, cols), BF16)
            kinds = jnp.broadcast_to(modality_ref[...].astype(F32), (16, rows))
            out[rows:, :rows] = kinds.astype(BF16)

    message = jax.ShapeDtypeStruct((rows + 16, cols), BF16)
    return pl.pallas_call(
        kernel,
        grid_spec=pltpu.PrefetchScalarGridSpec(
            num_scalar_prefetch=1,
            grid=(1,),
            in_specs=[whole_block((rows, width)), whole_block((1, rows))],
            out_specs=[whole_block(message.shape)] * members.shape[0],
        ),
        out_shape=[message] * members.shape[0],
        cost_estimate=cost(0, (tokens, tokens)),
        compiler_params=params(8),
    )(members, tokens, modality.reshape(1, rows))


def masked_send(pick, parts, text_rows):
    total, held = pick.shape
    rows = held // len(parts)
    cols = parts[0].shape[1]
    tile = total // 4

    def kernel(pick_ref, *refs):
        part_refs, out_ref, values, kinds = refs[: len(parts)], refs[-3], refs[-2], refs[-1]
        step = pl.program_id(0)

        @pl.when(step == 0)
        def _():
            for d, ref in enumerate(part_refs):
                values[d * rows : (d + 1) * rows, :] = ref[:rows, :]
                kinds[:, d * rows : (d + 1) * rows] = ref[rows:, :rows]

        kind = kinds[:1, :].astype(F32)
        row = step * tile + lax.broadcasted_iota(jnp.int32, (tile, 1), 0)
        keep = jnp.where(row < text_rows, 1.0 - kind, kind)
        chosen = (pick_ref[...].astype(F32) * keep).astype(BF16)
        out_ref[...] = dot(chosen, values[...], ROW_COL).astype(BF16)

    return pl.pallas_call(
        kernel,
        grid=(4,),
        out_shape=kept((total, cols), BF16),
        in_specs=[pl.BlockSpec((tile, held), lambda i: (i, 0))]
        + [pl.BlockSpec(part.shape, lambda i: (0, 0)) for part in parts],
        out_specs=pl.BlockSpec((tile, cols), lambda i: (i, 0)),
        scratch_shapes=[pltpu.VMEM((held, cols), BF16), pltpu.VMEM((16, held), BF16)],
        cost_estimate=pl.CostEstimate(
            flops=2 * total * held * cols, bytes_accessed=2 * (total * cols * 2 + total * held), transcendentals=0
        ),
        compiler_params=params(8),
    )(pick, *parts)


def assemble(parts, members, dtype, rows):
    cols = parts[0].shape[1]

    def kernel(members_ref, *refs):
        for d, ref in enumerate(refs[:-1]):
            start = pl.multiple_of(members_ref[d] * cols, 128)
            refs[-1][:, pl.ds(start, cols)] = ref[...].astype(dtype)

    return pl.pallas_call(
        kernel,
        grid_spec=pltpu.PrefetchScalarGridSpec(
            num_scalar_prefetch=1,
            grid=(2,),
            in_specs=[pl.BlockSpec((rows // 2, cols), lambda i, m: (i, 0)) for _ in parts],
            out_specs=pl.BlockSpec((rows // 2, len(parts) * cols), lambda i, m: (i, 0)),
        ),
        out_shape=jax.ShapeDtypeStruct((rows, len(parts) * cols), dtype),
        cost_estimate=pl.CostEstimate(
            flops=0, bytes_accessed=len(parts) * rows * cols * (2 + jnp.dtype(dtype).itemsize), transcendentals=0
        ),
        compiler_params=params(10),
    )(members, *parts)


def weight_grads(inputs, members, gate_back, up_back):
    count, cols = inputs[0].shape
    share = gate_back.shape[1]
    blocks = [block if isinstance(block, tuple) else (block,) for block in inputs]
    pieces = [piece for block in blocks for piece in block]

    def kernel(members_ref, *refs):
        gate_ref, up_ref, gate_out, up_out = refs[-4:]
        refs = list(refs[: len(pieces)])
        for d, block in enumerate(blocks):
            held = [refs.pop(0) for _ in block]

            @pl.when(pl.program_id(0) == d)
            def _(held=held):
                for grad, out in ((gate_ref, gate_out), (up_ref, up_out)):
                    size = held[0].shape[0]
                    out[...] = sum(
                        dot(ref[...], grad[i * size : (i + 1) * size, :], ROW_ROW) for i, ref in enumerate(held)
                    )

    whole = jax.ShapeDtypeStruct((len(inputs) * cols, share), F32)
    return pl.pallas_call(
        kernel,
        grid_spec=pltpu.PrefetchScalarGridSpec(
            num_scalar_prefetch=1,
            grid=(len(inputs),),
            in_specs=[whole_block(piece.shape) for piece in pieces] + [whole_block((count, share))] * 2,
            out_specs=[pl.BlockSpec((cols, share), lambda d, m: (m[d], 0))] * 2,
        ),
        out_shape=[whole, whole],
        cost_estimate=pl.CostEstimate(
            flops=4 * count * cols * share * len(inputs),
            bytes_accessed=len(inputs) * (count * cols * 2 + cols * share * 8),
            transcendentals=0,
        ),
        compiler_params=params(16),
    )(members, *pieces, gate_back, up_back)


def fetch_rows(place_in, got):
    count, total = place_in.shape
    cols = got.shape[1]
    tile = cols // 4

    def kernel(place_ref, got_ref, out_ref):
        out_ref[...] = dot(place_ref[...], got_ref[...], ROW_COL).astype(BF16)

    return pl.pallas_call(
        kernel,
        grid=(4,),
        in_specs=[whole_block((count, total)), pl.BlockSpec((total, tile), lambda i: (0, i))],
        out_specs=pl.BlockSpec((count, tile), lambda i: (0, i)),
        out_shape=kept((count, cols), BF16),
        cost_estimate=cost(2 * count * total * cols, (place_in, got, place_in)),
        compiler_params=params(8),
    )(place_in, got)


def hidden_from(gate_sum, up_sum, far, w_gate, w_up, members):
    half, cols = far[0].shape
    count, share = gate_sum.shape

    def kernel(members_ref, gate_ref, up_ref, top, low, wg_ref, wu_ref, gate_out, up_out, hidden_out):
        for start, ref in ((0, top), (half, low)):
            span = slice(start, start + half)
            gate = gate_ref[span, :] + dot(ref[...], wg_ref[...], ROW_COL)
            up = up_ref[span, :] + dot(ref[...], wu_ref[...], ROW_COL)
            gate_out[span, :] = gate
            up_out[span, :] = up
            hidden_out[span, :] = (gate * jax.nn.sigmoid(gate) * up).astype(BF16)

    wide = kept((count, share), F32)
    return pl.pallas_call(
        kernel,
        grid_spec=pltpu.PrefetchScalarGridSpec(
            num_scalar_prefetch=1,
            grid=(1,),
            in_specs=[whole_block((count, share))] * 2
            + [whole_block((half, cols))] * 2
            + [pl.BlockSpec((cols, share), lambda i, m: (m[2], 0))] * 2,
            out_specs=[whole_block((count, share))] * 3,
        ),
        out_shape=[wide, wide, jax.ShapeDtypeStruct((count, share), BF16)],
        cost_estimate=cost(4 * count * cols * share, (gate_sum, up_sum, *far, gate_sum, up_sum)),
        compiler_params=params(8),
    )(members, gate_sum, up_sum, *far, w_gate, w_up)


def fetch_and_back(place_in, got, down_parts):
    count, total = place_in.shape
    share, cols = down_parts[0].shape
    tile = count // 2

    def kernel(place_ref, got_ref, *refs):
        downs, (rows_out, *back_out) = refs[: len(down_parts)], refs[len(down_parts) :]
        rows = dot(place_ref[...], got_ref[...], ROW_COL).astype(BF16)
        rows_out[...] = rows
        for down, out in zip(downs, back_out):
            out[...] = dot(rows, down[...], COL_COL).astype(out.dtype)

    kinds = [F32] + [BF16] * (len(down_parts) - 1)
    return pl.pallas_call(
        kernel,
        grid=(2,),
        in_specs=[pl.BlockSpec((tile, total), lambda i: (i, 0)), whole_block(got.shape)]
        + [whole_block((share, cols))] * len(down_parts),
        out_specs=[pl.BlockSpec((tile, cols), lambda i: (i, 0))]
        + [pl.BlockSpec((tile, share), lambda i: (i, 0))] * len(kinds),
        out_shape=[kept((count, cols), BF16)]
        + [jax.ShapeDtypeStruct((count, share), kind) for kind in kinds],
        cost_estimate=cost(2 * count * total * cols + 8 * count * share * cols, (place_in, got, *down_parts)),
        compiler_params=params(14),
    )(*from_hbm(place_in, got, *down_parts))


def weighted_slots(hidden_parts, down_parts, weight, place_out):
    total, count = place_out.shape
    share, cols = down_parts[0].shape
    tile = cols // 4
    pieces = len(hidden_parts)

    def kernel(*refs):
        hiddens, downs = refs[:pieces], refs[pieces : 2 * pieces]
        weight_ref, place_ref, slots_out = refs[2 * pieces :]
        hidden = jnp.concatenate([ref[...] for ref in hiddens], axis=1)
        out = dot(hidden, jnp.concatenate([ref[...] for ref in downs], axis=0), ROW_COL)
        slots_out[...] = dot(place_ref[...], (weight_ref[...] * out).astype(BF16), ROW_COL).astype(BF16)

    return pl.pallas_call(
        kernel,
        grid=(4,),
        in_specs=[whole_block((count, share))] * pieces
        + [pl.BlockSpec((share, tile), lambda i: (0, i))] * pieces
        + [whole_block((count, 1)), whole_block((total, count))],
        out_specs=pl.BlockSpec((total, tile), lambda i: (0, i)),
        out_shape=kept((total, cols), BF16),
        cost_estimate=cost(
            2 * count * cols * (total + pieces * share), (*hidden_parts, *down_parts, place_out, place_out)
        ),
        compiler_params=params(10),
    )(*hidden_parts, *down_parts, weight, place_out)


def first_hop(back_parts, hidden, gate_pre, up_pre, weight, w_gate, w_up, order):
    count, share = gate_pre.shape
    half = count // 2
    cols = w_gate.shape[0] // (len(order) + 1)
    pieces = len(back_parts)

    def kernel(order_ref, *refs):
        hidden_ref, gate_ref, up_ref, weight_ref, wg_ref, wu_ref = refs[pieces : pieces + 6]
        gate_out, up_out, rise_out, fall_out, sum_out = refs[pieces + 6 :]
        step = pl.program_id(0)

        @pl.when(step == 0)
        def _():
            back = add(*(ref[...] for ref in refs[:pieces]))
            sum_out[...] = jnp.sum(hidden_ref[...].astype(F32) * back, axis=1, keepdims=True)
            back = weight_ref[...] * back
            gate = gate_ref[...]
            sig = jax.nn.sigmoid(gate)
            gate_out[...] = (back * up_ref[...] * (sig * (1.0 + gate * (1.0 - sig)))).astype(BF16)
            up_out[...] = (back * (gate * sig)).astype(BF16)

        def product(start, stop):
            grads = jnp.concatenate([gate_out[start:stop, :], up_out[start:stop, :]], axis=1)
            weights = jnp.concatenate([wg_ref[...], wu_ref[...]], axis=1)
            return dot(grads, weights, COL_COL).astype(BF16)

        @pl.when(step == 0)
        def _():
            rows = product(0, count)
            rise_out[:half, :] = rows[:half]
            fall_out[half:, :] = rows[half:]

        @pl.when(step == 1)
        def _():
            rise_out[half:, :] = product(half, count)

        @pl.when(step == 2)
        def _():
            fall_out[:half, :] = product(0, half)

    small = kept((count, share), BF16)
    wide = kept((count, cols), BF16)
    return pl.pallas_call(
        kernel,
        grid_spec=pltpu.PrefetchScalarGridSpec(
            num_scalar_prefetch=1,
            grid=(len(order),),
            in_specs=[whole_block((count, share))] * (pieces + 3)
            + [whole_block((count, 1))]
            + [pl.BlockSpec((cols, share), lambda j, m: (m[j], 0))] * 2,
            out_specs=[whole_block((count, share))] * 2
            + [whole_block((count, cols))] * 2
            + [whole_block((count, 1))],
        ),
        out_shape=[small, small, wide, wide, kept((count, 1), F32)],
        cost_estimate=cost(8 * count * share * cols, (*back_parts, gate_pre, up_pre, w_gate, w_up)),
        compiler_params=params(16),
    )(jnp.stack(order).astype(jnp.int32), *back_parts, hidden, *from_hbm(gate_pre, up_pre, weight, w_gate, w_up))


def summed_slots(own, rise, fall, rise_last, fall_last, place_out):
    total, count = place_out.shape
    half, cols = rise_last.shape
    tile = cols // 4

    def kernel(own_ref, rise_ref, fall_ref, rise_last_ref, fall_last_ref, place_ref, out_ref):
        top = add(own_ref[:half, :], rise_last_ref[...], fall_ref[...])
        low = add(own_ref[half:, :], rise_ref[...], fall_last_ref[...])
        sums = jnp.concatenate([top, low], axis=0).astype(BF16)
        out_ref[...] = dot(place_ref[...], sums, ROW_COL).astype(BF16)

    return pl.pallas_call(
        kernel,
        grid=(4,),
        in_specs=[
            pl.BlockSpec((count, tile), lambda i: (0, i)),
            pl.BlockSpec((half, tile), lambda i: (1, i)),
            pl.BlockSpec((half, tile), lambda i: (0, i)),
            pl.BlockSpec((half, tile), lambda i: (0, i)),
            pl.BlockSpec((half, tile), lambda i: (0, i)),
            whole_block((total, count)),
        ],
        out_specs=pl.BlockSpec((total, tile), lambda i: (0, i)),
        out_shape=kept((total, cols), BF16),
        cost_estimate=cost(2 * total * count * cols, (own, rise, fall, place_out, place_out)),
        compiler_params=params(10),
    )(own, rise, fall, rise_last, fall_last, place_out)


def body(tokens, modality, chosen, gates, w_gate, w_up, w_down, cotangent):
    tok_rows, width = tokens.shape
    size = lax.axis_size("pool")
    ep_size = lax.axis_size("ep")
    slots = 2 * tok_rows // ep_size
    capacity = chosen.shape[1]
    text_count = 3 * ep_size // 4
    cols = width // size
    share = w_gate.shape[2]
    me = lax.axis_index("pool")
    mine = lax.axis_index("ep")
    members = [(me + d) % size for d in range(size)]
    pool_order = jnp.stack(members).astype(jnp.int32)

    def columns(array):
        return lambda d: lax.dynamic_slice(
            array, (0, members[d % size] * cols), (array.shape[0], cols)
        )

    def rows(array, count):
        return lambda d: lax.dynamic_slice(
            array, (members[d % size] * count, 0), (count, array.shape[1])
        )

    messages = token_messages(tokens, modality, pool_order)
    token_parts = swap(lambda d: messages[d % size])
    cotangent = after(cotangent, *messages)
    later = token_parts[1:]
    grad_parts = swap(lambda d: after(columns(cotangent)(d), *later) if d == 2 else columns(cotangent)(d))
    down_parts = swap(lambda d: after(columns(w_down[0])(d), *later))

    token_at = []
    for d in range(size):
        first = (members[d] * ep_size + mine) * tok_rows
        local = chosen - first
        below = jnp.sum((local < 0).astype(jnp.int32), axis=1, keepdims=True)
        inside = (local >= 0) & (local < tok_rows)
        place = jnp.where(inside, jnp.arange(capacity, dtype=jnp.int32)[None, :] - below, -1)
        at_slot = place[:, None, :] == jnp.arange(slots, dtype=jnp.int32)[None, :, None]
        held = jnp.sum(jnp.where(at_slot, local[:, None, :] + 1, 0), axis=2) - 1
        token_at.append(jnp.where(held < 0, -1, held + d * tok_rows))
    token_at = jnp.stack(token_at, axis=1).reshape(ep_size * size * slots, 1)
    token_ids = jnp.arange(size * tok_rows, dtype=jnp.int32)
    pick = (token_at == token_ids[None, :]).astype(BF16)
    pick_back = (token_at.reshape(1, -1) == token_ids[:, None]).astype(BF16)
    pick, pick_back = lax.optimization_barrier((pick, pick_back))

    picks = lax.dynamic_slice_in_dim(chosen, mine, 1, 0)[0]
    holder = picks // tok_rows
    order = jnp.arange(capacity, dtype=jnp.int32)
    same = (holder[:, None] == holder[None, :]) & (order[None, :] < order[:, None])
    rank = jnp.sum(same.astype(jnp.int32), axis=1)
    pool_of, ep_of = holder // ep_size, holder % ep_size
    flat = (ep_of * size + (pool_of - me) % size) * slots + rank
    slot_total = ep_size * size * slots
    slot_ids = jnp.arange(slot_total, dtype=jnp.int32)
    place_in = (flat[:, None] == slot_ids[None, :]).astype(BF16)
    place_out = (flat[None, :] == slot_ids[:, None]).astype(BF16)
    place_in, place_out = lax.optimization_barrier((place_in, place_out))

    def exchange(values):
        blocks = values.reshape(ep_size, size * slots, cols)
        blocks = lax.all_to_all(blocks, "ep", split_axis=0, concat_axis=0, tiled=True)
        return blocks.reshape(slot_total, cols)

    def collect(got):
        return dot(pick_back, got, ROW_COL, BF16)

    def of_holder(summed, d):
        return summed[d % size * tok_rows : (d % size + 1) * tok_rows]

    wg, wu = w_gate[0], w_up[0]
    weight = gates[0][:, None]
    sent = masked_send(pick, token_parts, text_count * size * slots)
    sent_grads = dot(pick, jnp.concatenate(grad_parts, axis=0), ROW_COL, BF16)
    block = fetch_rows(place_in, after(exchange(sent), sent_grads))
    inputs = ring_gather(block)
    got = exchange(after(sent_grads, block, *down_parts))

    def near_sum(weights):
        return sum(dot(inputs[d], rows(weights, cols)(d), ROW_COL) for d in (0, 1, 3))

    gate_pre, up_pre, hidden = hidden_from(near_sum(wg), near_sum(wu), inputs[2], wg, wu, pool_order)
    grads, *back_parts = fetch_and_back(place_in, got, down_parts)
    came = swap(lambda d: back_parts[d % size])
    hidden_parts = swap(lambda d: hidden)
    hidden_parts = lax.optimization_barrier((*hidden_parts, *back_parts))[:size]

    slots_out = weighted_slots(hidden_parts, down_parts, weight, place_out)
    came[1] = after(came[1], slots_out)
    gate_back, up_back, rise, fall, gate_sum = first_hop(
        came, hidden, gate_pre, up_pre, weight, wg, wu, [members[2], members[1], members[3]]
    )
    sent_first = rise, fall
    mixed_sum = collect(exchange(after(slots_out, *sent_first)))
    rise, fall = shift(rise, 1), shift(fall, -1)
    half = capacity // 2

    def share_in(d, span):
        gate, up = (after(grad, *sent_first)[span] for grad in (gate_back, up_back))
        return dot(gate, rows(wg, cols)(d), COL_COL) + dot(up, rows(wu, cols)(d), COL_COL)

    own = share_in(0, slice(None))
    behind = lax.optimization_barrier(share_in(3, slice(half, None)))
    hops = (
        (share_in(1, slice(0, half)) + rise[:half].astype(F32)).astype(BF16),
        add(behind, fall[half:]).astype(BF16),
    )
    last = shift(hops[0], 1), shift(hops[1], -1)
    slots_in = summed_slots(own, rise, fall, *last, place_out)
    got = exchange(slots_in)

    gate_sum = after(gate_sum, *hops).reshape(1, capacity)
    gate_rows = jnp.concatenate(thirds(gate_sum), axis=0)
    gate_rows = jnp.pad(gate_rows, ((0, 13), (0, cols - capacity)))
    mixed_parts = swap(lambda d: jnp.concatenate([of_holder(mixed_sum, d), gate_rows], axis=0))
    mixed = assemble(mixed_parts, pool_order, BF16, tok_rows)
    gate_parts = [part[tok_rows : tok_rows + 3, :capacity].astype(F32) for part in mixed_parts]
    gate_parts = [part[0:1] + part[1:2] + part[2:3] for part in gate_parts]
    gate_grad = (gate_parts[0] + gate_parts[2]) + (gate_parts[1] + gate_parts[3])
    hidden_all = jnp.concatenate(after(hidden_parts, *hops), axis=1)
    scaled = (weight * hidden_all.astype(F32)).astype(BF16)
    down_grad = dot(scaled, grads, ROW_ROW, BF16)

    def down_block(d):
        block = down_grad[d % size * share : (d % size + 1) * share]
        return after(block, *last) if d == 2 else block

    down_grad = swap(down_block)
    down_grad = [after(part, mixed_sum) for part in down_grad]
    wd_grad = assemble(down_grad, pool_order, F32, share)
    wg_grad, wu_grad = weight_grads(
        inputs, pool_order, after(gate_back, slots_in, mixed_sum), after(up_back, slots_in)
    )
    got = after(got, mixed, wd_grad, wg_grad, wu_grad, gate_grad)
    summed = collect(got)
    token_grad = assemble(swap(lambda d: of_holder(summed, d)), pool_order, BF16, tok_rows)
    return (mixed, token_grad, gate_grad, wg_grad[None], wu_grad[None], wd_grad[None])


def solution(mesh):
    return jax.shard_map(
        body,
        mesh=mesh,
        in_specs=(
            P(BOTH, None),
            P(BOTH),
            P(),
            P("ep", None),
            P("ep", None, "pool"),
            P("ep", None, "pool"),
            P("ep", "pool", None),
            P(BOTH, None),
        ),
        out_specs=(
            P(BOTH, None),
            P(BOTH, None),
            P("ep", None),
            P("ep", None, "pool"),
            P("ep", None, "pool"),
            P("ep", "pool", None),
        ),
        check_vma=False,
    )
```
